32 devices in a mesh: row: 8 (over y, x, core), rep: 4 (over z).
Axes of the slice: x: 2, y: 2, z: 4, core: 2. Of those that a mesh axis runs over, the one named last changes fastest.
Arguments:
- node_feats: bfloat16 [8192, 1024], P('row'), may hold values from -6 to 6
- block_cols: int32 [64, 4], P('row'), may hold values from -1 to 63, as said below
- block_vals: bfloat16 [64, 4, 128, 128], P('row'), may hold values from -0.26367188 to 0.26367188
- w_in: bfloat16 [1024, 4096], P(None, 'rep'), may hold values from -0.1875 to 0.1875
- w_out: bfloat16 [1024, 4096], P(None, 'rep'), may hold values from -0.09375 to 0.09375
- cotangent: bfloat16 [8192, 1024], P('row', 'rep'), may hold values from -6 to 6
Outputs:
- updated: bfloat16 [8192, 1024], P('row', 'rep')
- grad_nodes: bfloat16 [8192, 1024], P('row', 'rep')
The draws below stay inside these ranges and needn't reach their ends.
Inputs may be any that keep to these rules, and one draw needn't show every extreme that they name: `block_cols`: slot 0 of block-row b holds b itself. Every other present block-column lies within 16 block-rows of its block-row; absent slots hold -1, and the number of present blocks differs from block-row to block-row. A pair of block-row and block-column may repeat.
All inputs are finite; a program needn't handle non-finite values.
Results may differ from the reference program's by a relative error of at most 0.013.
Values may be sent and summed in bfloat16 or wider, within the bound.
A program may use at most 128 MiB of HBM per device.

```python
import jax
import jax.numpy as jnp
from jax import lax

D = 1024
HID = 4096
SLOTS = 4
ROWS_DEV = 1024
NODES = 8192
BLOCK_ROWS = 64
N_REP = 4


def draw_block_cols(key, part):
    reach = 2 * (ROWS_DEV // 128)
    grid_shape = (BLOCK_ROWS, SLOTS)
    block_rows = jnp.arange(BLOCK_ROWS, dtype=jnp.int32)[:, None]
    slot_ids = jnp.arange(SLOTS, dtype=jnp.int32)[None, :]
    key_mag = jax.random.fold_in(key, 11)
    key_sign = jax.random.fold_in(key, 12)
    key_live = jax.random.fold_in(key, 13)
    magnitude = jax.random.randint(key_mag, grid_shape, 1, reach + 1)
    signs = jax.random.randint(key_sign, grid_shape, 0, 2) * 2 - 1
    alive = jax.random.randint(key_live, grid_shape, 0, 10) < 7
    target = block_rows + magnitude * signs
    usable = alive & (target >= 0) & (target < BLOCK_ROWS)
    chosen = jnp.where(usable, target, -1)
    chosen = jnp.where(slot_ids == 0, block_rows, chosen)
    chosen = jnp.where((block_rows == 0) & (slot_ids == SLOTS - 1), -1, chosen)
    return chosen.astype(jnp.int32)


def block_scale(stream_key, shape, cuts, low, top_value):
    factor_of = 1.0
    for axis_at, blocks in cuts:
        steps = jax.random.uniform(jax.random.fold_in(jax.random.fold_in(stream_key, 6), axis_at), (blocks,), jnp.float32, low / len(cuts), top_value / len(cuts))
        factor_of = factor_of * jnp.repeat(jnp.exp(steps), shape[axis_at] // blocks).reshape((-1,) + (1,) * (len(shape) - 1 - axis_at))
    return factor_of


def scatter_about(stream_key, dims, spread, limit, split=(), held_as=jnp.bfloat16):
    drawn = spread * jax.random.normal(stream_key, dims, jnp.float32)
    if split:
        drawn = drawn * block_scale(stream_key, dims, split, -0.22, 0.18)
    return jnp.clip(drawn, -limit, limit).astype(held_as)


def setup_inputs(seed: int = 0) -> dict:
    key_of = jax.random.split(jax.random.key(seed), 7)
    node_feats = scatter_about(key_of[0], (NODES, D), 1.0, 6.0, ((0, 8),))
    block_cols = draw_block_cols(jax.random.fold_in(key_of[6], 71), 0)
    block_vals = scatter_about(key_of[2], (BLOCK_ROWS, SLOTS, 128, 128), ((SLOTS * 128) ** -0.5), 0.26367188, ((0, 8),))
    w_in = scatter_about(key_of[3], (D, HID), D ** -0.5, 0.1875, ((1, 4),))
    w_out = scatter_about(key_of[4], (D, HID), HID ** -0.5, 0.09375, ((1, 4),))
    cotangent = scatter_about(key_of[5], (NODES, D), 1.0, 6.0, ((0, 8), (1, 4)))
    return dict(node_feats=node_feats, block_cols=block_cols, block_vals=block_vals, w_in=w_in, w_out=w_out, cotangent=cotangent)


def gelu_value(values):
    cubic_arg = 0.7978845608 * (values + 0.044715 * values * values * values)
    return 0.5 * values * (1.0 + jnp.tanh(cubic_arg))


def gelu_slope(values):
    cubic_arg = 0.7978845608 * (values + 0.044715 * values * values * values)
    tangent = jnp.tanh(cubic_arg)
    return 0.5 * (1.0 + tangent) + 0.5 * values * (1.0 - tangent * tangent) * 0.7978845608 * (1.0 + 3.0 * 0.044715 * values * values)


def grouped_product(left, weight, groups):
    width = left.shape[1] // groups
    total = jnp.zeros((left.shape[0], weight.shape[0]), jnp.float32)
    for group in range(groups):
        part = jnp.dot(left[:, group * width:(group + 1) * width], weight[:, group * width:(group + 1) * width].T, preferred_element_type=jnp.float32)
        rounded = lax.optimization_barrier(part.astype(jnp.bfloat16))
        total = total + rounded.astype(jnp.float32)
    return total


def reference(node_feats, block_cols, block_vals, w_in, w_out, cotangent):
    block_count = block_cols.shape[0]
    feat_width = node_feats.shape[1]
    present = block_cols >= 0
    padded_index = jnp.where(present, block_cols + 2, 0).astype(jnp.int32)
    mask_f = present.astype(jnp.float32)[:, :, None, None]
    vals_f = block_vals.astype(jnp.float32)
    panels = node_feats.reshape(block_count, 128, feat_width).astype(jnp.float32)
    padded = jnp.pad(panels, ((2, 2), (0, 0), (0, 0)))
    picked = padded[padded_index] * mask_f
    agg = jnp.einsum("rsij,rsjf->rif", vals_f, picked).reshape(-1, feat_width).astype(jnp.bfloat16)
    pre_act = jnp.dot(agg, w_in, preferred_element_type=jnp.float32)
    hidden = gelu_value(pre_act).astype(jnp.bfloat16)
    branch_out = grouped_product(hidden, w_out, N_REP)
    updated = (node_feats.astype(jnp.float32) + branch_out).astype(jnp.bfloat16)
    grad_hidden = jnp.dot(cotangent, w_out, preferred_element_type=jnp.float32)
    grad_pre = (grad_hidden * gelu_slope(pre_act)).astype(jnp.bfloat16)
    adjoint = grouped_product(grad_pre, w_in, N_REP).astype(jnp.bfloat16)
    adjoint_blocks = adjoint.reshape(block_count, 128, feat_width).astype(jnp.float32)
    contrib = jnp.einsum("rsji,rjf->rsif", vals_f, adjoint_blocks) * mask_f
    landing = jnp.zeros((block_count + 4, 128, feat_width), jnp.float32)
    landing = landing.at[padded_index].add(contrib)
    transposed = landing[2:-2].reshape(-1, feat_width)
    grad_nodes = (cotangent.astype(jnp.float32) + transposed).astype(jnp.bfloat16)
    return updated, grad_nodes
```

```python
import functools

import jax
import jax.numpy as jnp
from jax import lax
from jax.experimental import pallas as pl
from jax.experimental.pallas import tpu as pltpu
from jax.sharding import PartitionSpec as P

F32 = jnp.float32
BF16 = jnp.bfloat16
MESH = pl.DeviceIdType.MESH


def dot(a, b, dims=((1,), (0,))):
    return lax.dot_general(a, b, (dims, ((), ())), preferred_element_type=F32)


def gelu_pair(v):
    c = 0.7978845608
    vv = v * v
    t = jnp.tanh(c * (v + 0.044715 * v * vv))
    half = 0.5 * (1.0 + t)
    value = v * half
    slope = half + 0.5 * v * (1.0 - t * t) * c * (1.0 + 3.0 * 0.044715 * vv)
    return value, slope


def kernel(
    n_row, n_rep, mask_ref, feats_ref, vals_ref, w_in_ref, w_out_ref, cot_ref,
    upd_ref, grad_ref,
    ext, vals_t, dense, dense_t, agg_acc, w2_in, w2_out, cot_full, agg, agg_full, hid, gp,
    adj_p, out_p, adj_in, out_in, adj, c_send, c_sib, c_nbr,
    loc_sem, f_send, f_recv, w_send, w_recv, a_send, a_recv, c_sends, c_recvs,
):
    r, z = lax.axis_index("row"), lax.axis_index("rep")
    k = lax.rem(r, 2)
    sib = r + 1 - 2 * k
    mate = z + 1 - 2 * lax.rem(z, 2)
    rows, quarter = cot_ref.shape
    half = rows // 2
    row_blocks = rows // 128
    slots = vals_ref.shape[1]
    feat = w_in_ref.shape[0]
    hidw = w_in_ref.shape[1]
    has_up, has_dn = r + 2 < n_row, r >= 2
    peers = [lax.rem(z + i, n_rep) for i in range(1, n_rep)]
    froms = [lax.rem(z + n_rep - i, n_rep) for i in range(1, n_rep)]

    def remote(src, dst, send, recv, dev):
        return pltpu.make_async_remote_copy(
            src_ref=src, dst_ref=dst, send_sem=send, recv_sem=recv, device_id=dev, device_id_type=MESH
        )

    def panel(ref, slot):
        return ref.at[pl.ds(pl.multiple_of(slot * rows, rows), rows)]

    def halves(ref, s):
        return ref.at[pl.ds(pl.multiple_of(s * half, half), half)]

    barrier = pltpu.get_barrier_semaphore()
    for zp in peers:
        pl.semaphore_signal(barrier, inc=1, device_id=(r, zp), device_id_type=MESH)
    pl.semaphore_signal(barrier, inc=1, device_id=(sib, z), device_id_type=MESH)

    @pl.when(has_up)
    def _():
        pl.semaphore_signal(barrier, inc=1, device_id=(r + 2, z), device_id_type=MESH)

    @pl.when(has_dn)
    def _():
        pl.semaphore_signal(barrier, inc=1, device_id=(r - 2, z), device_id_type=MESH)

    columns = pl.ds(pl.multiple_of(z * quarter, quarter), quarter)
    own_copy = pltpu.make_async_copy(feats_ref.at[:, columns], panel(ext, 2), loc_sem)
    own_copy.start()
    own_copy.wait()
    pl.semaphore_wait(barrier, n_rep + has_up.astype(jnp.int32) + has_dn.astype(jnp.int32))

    own = panel(ext, 2)
    f_up = remote(own, panel(ext, 0), f_send.at[0], f_recv.at[0], (r + 2, z))
    f_dn = remote(own, panel(ext, 4), f_send.at[1], f_recv.at[1], (r - 2, z))
    f_sib = remote(own, panel(ext, 1 + 2 * k), f_send.at[2], f_recv.at[2], (sib, z))
    f_fwd = remote(
        panel(ext, 4 - 4 * k), panel(ext, 3 - 2 * k), f_send.at[3], f_recv.at[3], (sib, z)
    )
    from_dn = remote(own, panel(ext, 0), f_send.at[0], f_recv.at[0], (r - 2, z))
    from_up = remote(own, panel(ext, 4), f_send.at[1], f_recv.at[1], (r + 2, z))
    from_sib = remote(own, panel(ext, 3 - 2 * k), f_send.at[2], f_recv.at[2], (sib, z))
    from_fwd = remote(own, panel(ext, 1 + 2 * k), f_send.at[3], f_recv.at[3], (sib, z))
    fwd_out = jnp.where(k == 0, r + 2 < n_row, r >= 2)
    fwd_in = jnp.where(k == 0, r >= 2, r + 2 < n_row)

    @pl.when(has_up)
    def _():
        f_up.start()

    @pl.when(has_dn)
    def _():
        f_dn.start()

    f_sib.start()
    cot_out = [
        remote(halves(cot_ref, lax.rem(zp, 2)), cot_full.at[z], a_send.at[0, i], a_recv.at[0, i], (r, zp))
        for i, zp in enumerate(peers)
    ]
    for copy in cot_out:
        copy.start()
    w_out1 = [
        remote(halves(src, k), halves(dst, k), w_send.at[i], w_recv.at[i], (r, mate))
        for i, (src, dst) in enumerate(((w_in_ref, w2_in), (w_out_ref, w2_out)))
    ]
    w_fwd = [
        remote(halves(dst, k), halves(dst, k), w_send.at[2 + i], w_recv.at[2 + i], (sib, z))
        for i, dst in enumerate((w2_in, w2_out))
    ]
    w_got = [
        remote(halves(dst, 1 - k), halves(dst, 1 - k), w_send.at[2 + i], w_recv.at[2 + i], (sib, z))
        for i, dst in enumerate((w2_in, w2_out))
    ]
    for copy in w_out1:
        copy.start()

    @pl.when(jnp.logical_not(has_dn))
    def _():
        ext[0:rows] = jnp.zeros((rows, quarter), BF16)

    @pl.when(jnp.logical_not(has_up))
    def _():
        ext[4 * rows : 5 * rows] = jnp.zeros((rows, quarter), BF16)

    @pl.when(r < 1)
    def _():
        ext[rows : 2 * rows] = jnp.zeros((rows, quarter), BF16)

    @pl.when(r + 1 >= n_row)
    def _():
        ext[3 * rows : 4 * rows] = jnp.zeros((rows, quarter), BF16)

    cot_full[z] = cot_ref[pl.ds(pl.multiple_of(lax.rem(z, 2) * half, half), half), :]

    def transpose_block(b, carry):
        for s in range(slots):
            vals_t[b, s] = vals_ref[b, s].astype(F32).T.astype(BF16)
        return carry

    lax.fori_loop(0, row_blocks, transpose_block, 0)

    def fill_dense(t, carry):
        at = pl.ds(pl.multiple_of(t * 128, 128), 128)
        for b in range(row_blocks):
            straight = jnp.zeros((8, 16, 128), BF16)
            turned = jnp.zeros((8, 16, 128), BF16)
            for s in range(slots):
                row = mask_ref[t, b * slots + s : b * slots + s + 1, :]
                keep = jnp.broadcast_to(row, (16, 128)).astype(BF16)[None]
                straight = straight + vals_ref[b, s].reshape(8, 16, 128) * keep
                turned = turned + vals_t[b, s].reshape(8, 16, 128) * keep
            dense[b * 128 : (b + 1) * 128, at] = straight.reshape(128, 128)
            dense_t[at, b * 128 : (b + 1) * 128] = turned.reshape(128, 128)
        return carry

    lax.fori_loop(0, 5 * row_blocks, fill_dense, 0)

    def gather(slot, first=False):
        inner = pl.ds(pl.multiple_of(slot * rows, rows), rows)

        def step(m, carry):
            at = pl.ds(pl.multiple_of(m * 256, 256), 256)
            part = dot(dense[at, inner], ext[inner, :])
            agg_acc[at, :] = part if first else agg_acc[at, :] + part
            return carry

        lax.fori_loop(0, rows // 256, step, 0)

    gather(2, True)
    from_sib.wait_recv()
    gather(3 - 2 * k)

    @pl.when(has_dn)
    def _():
        from_dn.wait_recv()

    @pl.when(has_up)
    def _():
        from_up.wait_recv()

    @pl.when(fwd_out)
    def _():
        f_fwd.start()

    gather(0)
    gather(4)

    @pl.when(fwd_in)
    def _():
        from_fwd.wait_recv()

    gather(1 + 2 * k)
    agg[...] = agg_acc[...].astype(BF16)
    agg_out = [
        remote(halves(agg, lax.rem(zp, 2)), agg_full.at[z], a_send.at[1, i], a_recv.at[1, i], (r, zp))
        for i, zp in enumerate(peers)
    ]
    for copy in agg_out:
        copy.start()
    agg_full[z] = agg[pl.ds(pl.multiple_of(lax.rem(z, 2) * half, half), half), :]

    def arrivals(buf, kind):
        return [
            remote(buf.at[zf], buf.at[zf], a_send.at[kind, i], a_recv.at[kind, i], (r, zf))
            for i, zf in enumerate(froms)
        ]

    for copy in arrivals(cot_full, 0) + arrivals(agg_full, 1):
        copy.wait_recv()

    tile = 256

    def hidden_part(w_a, w_b, base):
        def step(i, carry):
            hc = pl.ds(pl.multiple_of(i * tile, tile), tile)
            to = pl.ds(pl.multiple_of(base + i * tile, tile), tile)
            wa, wb = w_a[:, hc], w_b[:, hc]
            for m in range(half // tile):
                rs = slice(m * tile, (m + 1) * tile)
                x = jnp.concatenate([agg_full[q, rs] for q in range(n_rep)], axis=1)
                c = jnp.concatenate([cot_full[q, rs] for q in range(n_rep)], axis=1)
                value, slope = gelu_pair(dot(x, wa))
                hid[rs, to] = value.astype(BF16)
                gp[rs, to] = (dot(c, wb) * slope).astype(BF16)
            return carry

        lax.fori_loop(0, hidw // tile, step, 0)

    hidden_part(w_in_ref, w_out_ref, 0)
    for copy, fwd in zip(w_out1, w_fwd):
        copy.wait_recv()
        fwd.start()
    for copy in w_got:
        copy.wait_recv()
    hidden_part(w2_in, w2_out, hidw)

    def product(src, w_a, w_b, dst, zq):
        at = pl.ds(pl.multiple_of(zq * quarter, quarter), quarter)
        wa, wb = w_a[at, :], w_b[at, :]
        for m in range(half // tile):
            rs = slice(m * tile, (m + 1) * tile)
            res = dot(src[rs, :hidw], wa, ((1,), (1,))) + dot(src[rs, hidw:], wb, ((1,), (1,)))
            dst[zq, rs] = res.astype(BF16)

    def spread(src, w_a, w_b, part, landing, kind):
        sent = []
        for i, zp in enumerate(peers):
            product(src, w_a, w_b, part, zp)
            copy = remote(
                part.at[zp], landing.at[z], a_send.at[kind, i], a_recv.at[kind, i], (r, zp)
            )
            copy.start()
            sent.append(copy)
        product(src, w_a, w_b, part, z)
        landing[z] = part[z]
        return sent

    adj_out = spread(gp, w_in_ref, w2_in, adj_p, adj_in, 2)
    out_out = spread(hid, w_out_ref, w2_out, out_p, out_in, 3)

    for copy in arrivals(adj_in, 2):
        copy.wait_recv()
    for s in range(2):
        total = adj_in[s].astype(F32)
        for q in range(s + 2, n_rep, 2):
            total = total + adj_in[q].astype(F32)
        adj[s * half : (s + 1) * half] = total.astype(BF16)

    def piece(p, m):
        at = pl.ds(pl.multiple_of(p * rows + m * tile, tile), tile)
        return dot(dense_t[at, :], adj[...])

    def put(p, slot):
        def step(m, carry):
            at = pl.ds(pl.multiple_of(m * tile, tile), tile)
            c_send[slot, at, :] = piece(p, m).astype(BF16)
            return carry

        lax.fori_loop(0, rows // tile, step, 0)

    plain_to, helped_to = r - 2 + 4 * k, r + 2 - 4 * k
    c_help = remote(c_send.at[0], c_sib.at[0], c_sends.at[0], c_recvs.at[0], (sib, z))
    c_own = remote(c_send.at[1], c_sib.at[1], c_sends.at[1], c_recvs.at[1], (sib, z))
    c_plain = remote(
        c_send.at[2], c_nbr.at[1 - k], c_sends.at[2], c_recvs.at[3 - k], (plain_to, z)
    )
    c_helped = remote(
        c_send.at[3], c_nbr.at[k], c_sends.at[3], c_recvs.at[2 + k], (helped_to, z)
    )
    put(1 + 2 * k, 0)
    c_help.start()
    put(4 * k, 2)
    plain_ok, helped_ok = fwd_in, fwd_out

    @pl.when(plain_ok)
    def _():
        c_plain.start()

    c_help.wait_recv()

    def add_help(m, carry):
        at = pl.ds(pl.multiple_of(m * tile, tile), tile)
        total = piece(4 - 4 * k, m) + c_sib[0, at, :].astype(F32)
        c_send[3, at, :] = total.astype(BF16)
        return carry

    lax.fori_loop(0, rows // tile, add_help, 0)

    @pl.when(helped_ok)
    def _():
        c_helped.start()

    put(3 - 2 * k, 1)
    c_own.start()

    for copy in arrivals(out_in, 3):
        copy.wait_recv()
    for s in range(2):
        total = out_in[s].astype(F32)
        for q in range(s + 2, n_rep, 2):
            total = total + out_in[q].astype(F32)
        mine = ext[2 * rows + s * half : 2 * rows + (s + 1) * half]
        upd_ref[s * half : (s + 1) * half] = (mine.astype(F32) + total).astype(BF16)

    c_own.wait_recv()
    from_low = remote(c_nbr.at[0], c_nbr.at[0], c_sends.at[2], c_recvs.at[2], (r - 2, z))
    from_high = remote(c_nbr.at[1], c_nbr.at[1], c_sends.at[3], c_recvs.at[3], (r + 2, z))

    @pl.when(has_dn)
    def _():
        from_low.wait_recv()

    @pl.when(jnp.logical_not(has_dn))
    def _():
        c_nbr[0] = jnp.zeros((rows, quarter), BF16)

    @pl.when(has_up)
    def _():
        from_high.wait_recv()

    @pl.when(jnp.logical_not(has_up))
    def _():
        c_nbr[1] = jnp.zeros((rows, quarter), BF16)

    def finish(m, carry):
        at = pl.ds(pl.multiple_of(m * tile, tile), tile)
        total = piece(2, m) + c_sib[1, at, :].astype(F32)
        total = total + c_nbr[0, at, :].astype(F32) + c_nbr[1, at, :].astype(F32)
        grad_ref[at, :] = (cot_ref[at, :].astype(F32) + total).astype(BF16)
        return carry

    lax.fori_loop(0, rows // tile, finish, 0)

    for copy in cot_out + w_out1 + w_fwd + agg_out + adj_out + out_out + [f_sib, c_help, c_own]:
        copy.wait_send()
    for ok, copy in (
        (has_up, f_up), (has_dn, f_dn), (fwd_out, f_fwd), (plain_ok, c_plain), (helped_ok, c_helped)
    ):
        pl.when(ok)(copy.wait_send)


def body(n_row, n_rep, node_feats, block_cols, block_vals, w_in, w_out, cotangent):
    rows, quarter = cotangent.shape
    feat = node_feats.shape[1]
    row_blocks, slots = block_cols.shape
    hidw = w_in.shape[1]
    half = rows // 2
    first = (lax.axis_index("row") - 2) * row_blocks
    position = jnp.where(block_cols >= 0, block_cols - first, -1).reshape(1, -1, 1)
    landing = jnp.arange(5 * row_blocks, dtype=jnp.int32).reshape(-1, 1, 1)
    mask = jnp.broadcast_to(
        (position == landing).astype(F32), (5 * row_blocks, row_blocks * slots, 128)
    )
    vmem = pl.BlockSpec(memory_space=pltpu.VMEM)
    dma = pltpu.SemaphoreType.DMA
    return pl.pallas_call(
        functools.partial(kernel, n_row, n_rep),
        out_shape=(jax.ShapeDtypeStruct((rows, quarter), BF16),) * 2,
        in_specs=[vmem, pl.BlockSpec(memory_space=pl.ANY), vmem, vmem, vmem, vmem],
        out_specs=(vmem, vmem),
        scratch_shapes=[
            pltpu.VMEM((5 * rows, quarter), BF16),
            pltpu.VMEM((row_blocks, slots, 128, 128), BF16),
            pltpu.VMEM((rows, 5 * rows), BF16),
            pltpu.VMEM((5 * rows, rows), BF16),
            pltpu.VMEM((rows, quarter), F32),
            pltpu.VMEM((feat, hidw), BF16),
            pltpu.VMEM((feat, hidw), BF16),
            pltpu.VMEM((n_rep, half, quarter), BF16),
            pltpu.VMEM((rows, quarter), BF16),
            pltpu.VMEM((n_rep, half, quarter), BF16),
            pltpu.VMEM((half, 2 * hidw), BF16),
            pltpu.VMEM((half, 2 * hidw), BF16),
            pltpu.VMEM((n_rep, half, quarter), BF16),
            pltpu.VMEM((n_rep, half, quarter), BF16),
            pltpu.VMEM((n_rep, half, quarter), BF16),
            pltpu.VMEM((n_rep, half, quarter), BF16),
            pltpu.VMEM((rows, quarter), BF16),
            pltpu.VMEM((4, rows, quarter), BF16),
            pltpu.VMEM((2, rows, quarter), BF16),
            pltpu.VMEM((2, rows, quarter), BF16),
            dma,
            dma((4,)),
            dma((4,)),
            dma((4,)),
            dma((4,)),
            dma((4, n_rep - 1)),
            dma((4, n_rep - 1)),
            dma((4,)),
            dma((4,)),
        ],
        compiler_params=pltpu.CompilerParams(
            collective_id=0, has_side_effects=True, vmem_limit_bytes=60 * 1024 * 1024
        ),
    )(mask, node_feats, block_vals, w_in, w_out, cotangent)


def solution(mesh):
    in_specs = (
        P("row", None),
        P("row", None),
        P("row", None, None, None),
        P(None, "rep"),
        P(None, "rep"),
        P("row", "rep"),
    )
    out_specs = (P("row", "rep"), P("row", "rep"))
    run = functools.partial(body, mesh.shape["row"], mesh.shape["rep"])
    return jax.shard_map(run, mesh=mesh, in_specs=in_specs, out_specs=out_specs, check_vma=False)
```

```python
import functools

import jax
import jax.numpy as jnp
from jax import lax
from jax.experimental import pallas as pl
from jax.experimental.pallas import tpu as pltpu
from jax.sharding import PartitionSpec as P

F32 = jnp.float32
BF16 = jnp.bfloat16
MESH = pl.DeviceIdType.MESH


def dot(a, b, dims=((1,), (0,))):
    return lax.dot_general(a, b, (dims, ((), ())), preferred_element_type=F32)


def gelu_pair(v):
    c = 0.7978845608
    vv = v * v
    t = jnp.tanh(c * (v + 0.044715 * v * vv))
    half = 0.5 * (1.0 + t)
    value = v * half
    slope = half + 0.5 * v * (1.0 - t * t) * c * (1.0 + 3.0 * 0.044715 * vv)
    return value, slope


def kernel(
    n_row, n_rep, mask_ref, feats_ref, vals_ref, w_in_ref, w_out_ref, cot_ref,
    upd_ref, grad_ref,
    ext, vals_t, dense, dense_t, agg_acc, w2_in, w2_out, cot_full, agg, agg_full, hid, gp,
    adj_p, out_p, adj_in, out_in, adj, c_send, c_sib, c_nbr,
    loc_sem, f_send, f_recv, w_send, w_recv, a_send, a_recv, c_sends, c_recvs,
):
    r, z = lax.axis_index("row"), lax.axis_index("rep")
    k = lax.rem(r, 2)
    sib = r + 1 - 2 * k
    mate = z + 1 - 2 * lax.rem(z, 2)
    bit2, bit4 = lax.rem(lax.div(r, 2), 2), lax.rem(lax.div(r, 4), 2)
    near, far = r + 2 - 4 * bit2, r + 4 - 8 * bit4
    rows, quarter = cot_ref.shape
    half = rows // 2
    row_blocks = rows // 128
    slots = vals_ref.shape[1]
    feat = w_in_ref.shape[0]
    hidw = w_in_ref.shape[1]
    has_up, has_dn = r + 2 < n_row, r >= 2
    peers = [lax.rem(z + i, n_rep) for i in range(1, n_rep)]
    froms = [lax.rem(z + n_rep - i, n_rep) for i in range(1, n_rep)]

    def remote(src, dst, send, recv, dev):
        return pltpu.make_async_remote_copy(
            src_ref=src, dst_ref=dst, send_sem=send, recv_sem=recv, device_id=dev, device_id_type=MESH
        )

    def panel(ref, slot):
        return ref.at[pl.ds(pl.multiple_of(slot * rows, rows), rows)]

    def halves(ref, s):
        return ref.at[pl.ds(pl.multiple_of(s * half, half), half)]

    barrier = pltpu.get_barrier_semaphore()
    for zp in peers:
        pl.semaphore_signal(barrier, inc=1, device_id=(r, zp), device_id_type=MESH)
    pl.semaphore_signal(barrier, inc=1, device_id=(sib, z), device_id_type=MESH)

    pl.semaphore_signal(barrier, inc=1, device_id=(far, z), device_id_type=MESH)

    @pl.when(has_up)
    def _():
        pl.semaphore_signal(barrier, inc=1, device_id=(r + 2, z), device_id_type=MESH)

    @pl.when(has_dn)
    def _():
        pl.semaphore_signal(barrier, inc=1, device_id=(r - 2, z), device_id_type=MESH)

    columns = pl.ds(pl.multiple_of(z * quarter, quarter), quarter)
    own_copy = pltpu.make_async_copy(feats_ref.at[:, columns], panel(ext, 2), loc_sem)
    own_copy.start()
    own_copy.wait()
    pl.semaphore_wait(barrier, n_rep + 1 + has_up.astype(jnp.int32) + has_dn.astype(jnp.int32))

    own = panel(ext, 2)
    f_up = remote(own, panel(ext, 0), f_send.at[0], f_recv.at[0], (r + 2, z))
    f_dn = remote(own, panel(ext, 4), f_send.at[1], f_recv.at[1], (r - 2, z))
    f_sib = remote(own, panel(ext, 1 + 2 * k), f_send.at[2], f_recv.at[2], (sib, z))
    f_fwd = remote(
        panel(ext, 4 - 4 * k), panel(ext, 3 - 2 * k), f_send.at[3], f_recv.at[3], (sib, z)
    )
    from_dn = remote(own, panel(ext, 0), f_send.at[0], f_recv.at[0], (r - 2, z))
    from_up = remote(own, panel(ext, 4), f_send.at[1], f_recv.at[1], (r + 2, z))
    from_sib = remote(own, panel(ext, 3 - 2 * k), f_send.at[2], f_recv.at[2], (sib, z))
    from_fwd = remote(own, panel(ext, 1 + 2 * k), f_send.at[3], f_recv.at[3], (sib, z))
    fwd_out = jnp.where(k == 0, r + 2 < n_row, r >= 2)
    fwd_in = jnp.where(k == 0, r >= 2, r + 2 < n_row)

    @pl.when(has_up)
    def _():
        f_up.start()

    @pl.when(has_dn)
    def _():
        f_dn.start()

    f_sib.start()
    cot_out = [
        remote(halves(cot_ref, lax.rem(zp, 2)), cot_full.at[z], a_send.at[0, i], a_recv.at[0, i], (r, zp))
        for i, zp in enumerate(peers)
    ]
    eighth = feat // 8
    quad, pair = 4 * k, 4 * k + 2 * bit2

    def span(ref, start, count):
        return ref.at[pl.ds(pl.multiple_of(start * eighth, eighth), count * eighth)]

    def round_of(step, start, count, dev, first=False):
        ends = ((w_in_ref if first else w2_in, w2_in), (w_out_ref if first else w2_out, w2_out))
        return [
            remote(
                span(src, start, count), span(dst, start, count),
                w_send.at[2 * step + i], w_recv.at[2 * step + i], dev,
            )
            for i, (src, dst) in enumerate(ends)
        ]

    w_rounds = [
        round_of(0, pair + bit4, 1, (r, mate), True),
        round_of(1, pair + bit4, 1, (far, z)),
        round_of(2, pair, 2, (near, z)),
        round_of(3, quad, 4, (sib, z)),
    ]
    w_lands = [
        w_rounds[0],
        round_of(1, pair + 1 - bit4, 1, (far, z)),
        round_of(2, quad + 2 - 2 * bit2, 2, (near, z)),
        round_of(3, 4 - quad, 4, (sib, z)),
    ]

    def pass_weights(step):
        if step:
            for copy in w_lands[step - 1]:
                copy.wait_recv()
        if step < 4:
            for copy in w_rounds[step]:
                copy.start()

    pass_weights(0)

    @pl.when(jnp.logical_not(has_dn))
    def _():
        ext[0:rows] = jnp.zeros((rows, quarter), BF16)

    @pl.when(jnp.logical_not(has_up))
    def _():
        ext[4 * rows : 5 * rows] = jnp.zeros((rows, quarter), BF16)

    @pl.when(r < 1)
    def _():
        ext[rows : 2 * rows] = jnp.zeros((rows, quarter), BF16)

    @pl.when(r + 1 >= n_row)
    def _():
        ext[3 * rows : 4 * rows] = jnp.zeros((rows, quarter), BF16)

    cot_full[z] = cot_ref[pl.ds(pl.multiple_of(lax.rem(z, 2) * half, half), half), :]

    def transpose_block(b, carry):
        for s in range(slots):
            vals_t[b, s] = vals_ref[b, s].astype(F32).T.astype(BF16)
        return carry

    lax.fori_loop(0, row_blocks, transpose_block, 0)

    def fill_dense(t, carry):
        at = pl.ds(pl.multiple_of(t * 128, 128), 128)
        for b in range(row_blocks):
            straight = jnp.zeros((8, 16, 128), BF16)
            turned = jnp.zeros((8, 16, 128), BF16)
            for s in range(slots):
                row = mask_ref[t, b * slots + s : b * slots + s + 1, :]
                keep = jnp.broadcast_to(row, (16, 128)).astype(BF16)[None]
                straight = straight + vals_ref[b, s].reshape(8, 16, 128) * keep
                turned = turned + vals_t[b, s].reshape(8, 16, 128) * keep
            dense[b * 128 : (b + 1) * 128, at] = straight.reshape(128, 128)
            dense_t[at, b * 128 : (b + 1) * 128] = turned.reshape(128, 128)
        return carry

    lax.fori_loop(0, 5 * row_blocks, fill_dense, 0)
    pass_weights(1)
    for copy in cot_out:
        copy.start()

    def gather(slot, first=False):
        inner = pl.ds(pl.multiple_of(slot * rows, rows), rows)

        def step(m, carry):
            at = pl.ds(pl.multiple_of(m * 256, 256), 256)
            part = dot(dense[at, inner], ext[inner, :])
            agg_acc[at, :] = part if first else agg_acc[at, :] + part
            return carry

        lax.fori_loop(0, rows // 256, step, 0)

    gather(2, True)
    from_sib.wait_recv()
    gather(3 - 2 * k)

    @pl.when(has_dn)
    def _():
        from_dn.wait_recv()

    @pl.when(has_up)
    def _():
        from_up.wait_recv()

    @pl.when(fwd_out)
    def _():
        f_fwd.start()

    pass_weights(2)
    gather(0)
    gather(4)

    @pl.when(fwd_in)
    def _():
        from_fwd.wait_recv()

    gather(1 + 2 * k)
    agg[...] = agg_acc[...].astype(BF16)
    agg_out = [
        remote(halves(agg, lax.rem(zp, 2)), agg_full.at[z], a_send.at[1, i], a_recv.at[1, i], (r, zp))
        for i, zp in enumerate(peers)
    ]
    for copy in agg_out:
        copy.start()
    agg_full[z] = agg[pl.ds(pl.multiple_of(lax.rem(z, 2) * half, half), half), :]

    def arrivals(buf, kind):
        return [
            remote(buf.at[zf], buf.at[zf], a_send.at[kind, i], a_recv.at[kind, i], (r, zf))
            for i, zf in enumerate(froms)
        ]

    pass_weights(3)
    for copy in arrivals(cot_full, 0) + arrivals(agg_full, 1):
        copy.wait_recv()

    tile = 256

    def hidden_part(w_a, w_b, base):
        def step(i, carry):
            hc = pl.ds(pl.multiple_of(i * tile, tile), tile)
            to = pl.ds(pl.multiple_of(base + i * tile, tile), tile)
            wa, wb = w_a[:, hc], w_b[:, hc]
            for m in range(half // tile):
                rs = slice(m * tile, (m + 1) * tile)
                x = jnp.concatenate([agg_full[q, rs] for q in range(n_rep)], axis=1)
                c = jnp.concatenate([cot_full[q, rs] for q in range(n_rep)], axis=1)
                value, slope = gelu_pair(dot(x, wa))
                hid[rs, to] = value.astype(BF16)
                gp[rs, to] = (dot(c, wb) * slope).astype(BF16)
            return carry

        lax.fori_loop(0, hidw // tile, step, 0)

    hidden_part(w_in_ref, w_out_ref, 0)
    pass_weights(4)
    hidden_part(w2_in, w2_out, hidw)

    def product(src, w_a, w_b, dst, zq):
        at = pl.ds(pl.multiple_of(zq * quarter, quarter), quarter)
        wa, wb = w_a[at, :], w_b[at, :]
        for m in range(half // tile):
            rs = slice(m * tile, (m + 1) * tile)
            res = dot(src[rs, :hidw], wa, ((1,), (1,))) + dot(src[rs, hidw:], wb, ((1,), (1,)))
            dst[zq, rs] = res.astype(BF16)

    def spread(src, w_a, w_b, part, landing, kind):
        sent = []
        for i, zp in enumerate(peers):
            product(src, w_a, w_b, part, zp)
            copy = remote(
                part.at[zp], landing.at[z], a_send.at[kind, i], a_recv.at[kind, i], (r, zp)
            )
            copy.start()
            sent.append(copy)
        product(src, w_a, w_b, part, z)
        landing[z] = part[z]
        return sent

    adj_out = spread(gp, w_in_ref, w2_in, adj_p, adj_in, 2)
    out_out = spread(hid, w_out_ref, w2_out, out_p, out_in, 3)

    for copy in arrivals(adj_in, 2):
        copy.wait_recv()
    for s in range(2):
        total = adj_in[s].astype(F32)
        for q in range(s + 2, n_rep, 2):
            total = total + adj_in[q].astype(F32)
        adj[s * half : (s + 1) * half] = total.astype(BF16)

    def piece(p, m):
        at = pl.ds(pl.multiple_of(p * rows + m * tile, tile), tile)
        return dot(dense_t[at, :], adj[...])

    def put(p, slot):
        def step(m, carry):
            at = pl.ds(pl.multiple_of(m * tile, tile), tile)
            c_send[slot, at, :] = piece(p, m).astype(BF16)
            return carry

        lax.fori_loop(0, rows // tile, step, 0)

    plain_to, helped_to = r - 2 + 4 * k, r + 2 - 4 * k
    c_help = remote(c_send.at[0], c_sib.at[0], c_sends.at[0], c_recvs.at[0], (sib, z))
    c_own = remote(c_send.at[1], c_sib.at[1], c_sends.at[1], c_recvs.at[1], (sib, z))
    c_plain = remote(
        c_send.at[2], c_nbr.at[1 - k], c_sends.at[2], c_recvs.at[3 - k], (plain_to, z)
    )
    c_helped = remote(
        c_send.at[3], c_nbr.at[k], c_sends.at[3], c_recvs.at[2 + k], (helped_to, z)
    )
    put(1 + 2 * k, 0)
    c_help.start()
    put(4 * k, 2)
    plain_ok, helped_ok = fwd_in, fwd_out

    @pl.when(plain_ok)
    def _():
        c_plain.start()

    c_help.wait_recv()

    def add_help(m, carry):
        at = pl.ds(pl.multiple_of(m * tile, tile), tile)
        total = piece(4 - 4 * k, m) + c_sib[0, at, :].astype(F32)
        c_send[3, at, :] = total.astype(BF16)
        return carry

    lax.fori_loop(0, rows // tile, add_help, 0)

    @pl.when(helped_ok)
    def _():
        c_helped.start()

    put(3 - 2 * k, 1)
    c_own.start()

    for copy in arrivals(out_in, 3):
        copy.wait_recv()
    for s in range(2):
        total = out_in[s].astype(F32)
        for q in range(s + 2, n_rep, 2):
            total = total + out_in[q].astype(F32)
        mine = ext[2 * rows + s * half : 2 * rows + (s + 1) * half]
        upd_ref[s * half : (s + 1) * half] = (mine.astype(F32) + total).astype(BF16)

    c_own.wait_recv()
    from_low = remote(c_nbr.at[0], c_nbr.at[0], c_sends.at[2], c_recvs.at[2], (r - 2, z))
    from_high = remote(c_nbr.at[1], c_nbr.at[1], c_sends.at[3], c_recvs.at[3], (r + 2, z))

    @pl.when(has_dn)
    def _():
        from_low.wait_recv()

    @pl.when(jnp.logical_not(has_dn))
    def _():
        c_nbr[0] = jnp.zeros((rows, quarter), BF16)

    @pl.when(has_up)
    def _():
        from_high.wait_recv()

    @pl.when(jnp.logical_not(has_up))
    def _():
        c_nbr[1] = jnp.zeros((rows, quarter), BF16)

    def finish(m, carry):
        at = pl.ds(pl.multiple_of(m * tile, tile), tile)
        total = piece(2, m) + c_sib[1, at, :].astype(F32)
        total = total + c_nbr[0, at, :].astype(F32) + c_nbr[1, at, :].astype(F32)
        grad_ref[at, :] = (cot_ref[at, :].astype(F32) + total).astype(BF16)
        return carry

    lax.fori_loop(0, rows // tile, finish, 0)

    for copy in cot_out + sum(w_rounds, []) + agg_out + adj_out + out_out + [f_sib, c_help, c_own]:
        copy.wait_send()
    for ok, copy in (
        (has_up, f_up), (has_dn, f_dn), (fwd_out, f_fwd), (plain_ok, c_plain), (helped_ok, c_helped)
    ):
        pl.when(ok)(copy.wait_send)


def body(n_row, n_rep, node_feats, block_cols, block_vals, w_in, w_out, cotangent):
    rows, quarter = cotangent.shape
    feat = node_feats.shape[1]
    row_blocks, slots = block_cols.shape
    hidw = w_in.shape[1]
    half = rows // 2
    first = (lax.axis_index("row") - 2) * row_blocks
    position = jnp.where(block_cols >= 0, block_cols - first, -1).reshape(1, -1, 1)
    landing = jnp.arange(5 * row_blocks, dtype=jnp.int32).reshape(-1, 1, 1)
    mask = jnp.broadcast_to(
        (position == landing).astype(F32), (5 * row_blocks, row_blocks * slots, 128)
    )
    vmem = pl.BlockSpec(memory_space=pltpu.VMEM)
    dma = pltpu.SemaphoreType.DMA
    return pl.pallas_call(
        functools.partial(kernel, n_row, n_rep),
        out_shape=(jax.ShapeDtypeStruct((rows, quarter), BF16),) * 2,
        in_specs=[vmem, pl.BlockSpec(memory_space=pl.ANY), vmem, vmem, vmem, vmem],
        out_specs=(vmem, vmem),
        scratch_shapes=[
            pltpu.VMEM((5 * rows, quarter), BF16),
            pltpu.VMEM((row_blocks, slots, 128, 128), BF16),
            pltpu.VMEM((rows, 5 * rows), BF16),
            pltpu.VMEM((5 * rows, rows), BF16),
            pltpu.VMEM((rows, quarter), F32),
            pltpu.VMEM((feat, hidw), BF16),
            pltpu.VMEM((feat, hidw), BF16),
            pltpu.VMEM((n_rep, half, quarter), BF16),
            pltpu.VMEM((rows, quarter), BF16),
            pltpu.VMEM((n_rep, half, quarter), BF16),
            pltpu.VMEM((half, 2 * hidw), BF16),
            pltpu.VMEM((half, 2 * hidw), BF16),
            pltpu.VMEM((n_rep, half, quarter), BF16),
            pltpu.VMEM((n_rep, half, quarter), BF16),
            pltpu.VMEM((n_rep, half, quarter), BF16),
            pltpu.VMEM((n_rep, half, quarter), BF16),
            pltpu.VMEM((rows, quarter), BF16),
            pltpu.VMEM((4, rows, quarter), BF16),
            pltpu.VMEM((2, rows, quarter), BF16),
            pltpu.VMEM((2, rows, quarter), BF16),
            dma,
            dma((4,)),
            dma((4,)),
            dma((8,)),
            dma((8,)),
            dma((4, n_rep - 1)),
            dma((4, n_rep - 1)),
            dma((4,)),
            dma((4,)),
        ],
        compiler_params=pltpu.CompilerParams(
            collective_id=0, has_side_effects=True, vmem_limit_bytes=60 * 1024 * 1024
        ),
    )(mask, node_feats, block_vals, w_in, w_out, cotangent)


def solution(mesh):
    in_specs = (
        P("row", None),
        P("row", None),
        P("row", None, None, None),
        P(None, "rep"),
        P(None, "rep"),
        P("row", "rep"),
    )
    out_specs = (P("row", "rep"), P("row", "rep"))
    run = functools.partial(body, mesh.shape["row"], mesh.shape["rep"])
    return jax.shard_map(run, mesh=mesh, in_specs=in_specs, out_specs=out_specs, check_vma=False)
```

```python
import functools

import jax
import jax.numpy as jnp
from jax import lax
from jax.experimental import pallas as pl
from jax.experimental.pallas import tpu as pltpu
from jax.sharding import PartitionSpec as P

F32 = jnp.float32
BF16 = jnp.bfloat16
MESH = pl.DeviceIdType.MESH


def dot(a, b, dims=((1,), (0,))):
    return lax.dot_general(a, b, (dims, ((), ())), preferred_element_type=F32)


def gelu_pair(v):
    c = 0.7978845608
    vv = v * v
    t = jnp.tanh(c * (v + 0.044715 * v * vv))
    half = 0.5 * (1.0 + t)
    value = v * half
    slope = half + 0.5 * v * (1.0 - t * t) * c * (1.0 + 3.0 * 0.044715 * vv)
    return value, slope


def kernel(
    n_row, n_rep, mask_ref, feats_ref, vals_ref, w_in_ref, w_out_ref, cot_ref,
    upd_ref, grad_ref,
    ext, vals_t, dense, dense_t, agg_acc, w2_in, w2_out, cot_full, agg, agg_full, hid, gp,
    adj_p, out_p, adj_in, out_in, adj, c_send, c_sib, c_nbr,
    loc_sem, f_send, f_recv, w_send, w_recv, a_send, a_recv, c_sends, c_recvs,
):
    r, z = lax.axis_index("row"), lax.axis_index("rep")
    k = lax.rem(r, 2)
    sib = r + 1 - 2 * k
    mate = z + 1 - 2 * lax.rem(z, 2)
    bit2, bit4 = lax.rem(lax.div(r, 2), 2), lax.rem(lax.div(r, 4), 2)
    near, far = r + 2 - 4 * bit2, r + 4 - 8 * bit4
    rows, quarter = cot_ref.shape
    half = rows // 2
    row_blocks = rows // 128
    slots = vals_ref.shape[1]
    feat = w_in_ref.shape[0]
    hidw = w_in_ref.shape[1]
    has_up, has_dn = r + 2 < n_row, r >= 2
    peers = [lax.rem(z + i, n_rep) for i in range(1, n_rep)]
    froms = [lax.rem(z + n_rep - i, n_rep) for i in range(1, n_rep)]

    def remote(src, dst, send, recv, dev):
        return pltpu.make_async_remote_copy(
            src_ref=src, dst_ref=dst, send_sem=send, recv_sem=recv, device_id=dev, device_id_type=MESH
        )

    def panel(ref, slot):
        return ref.at[pl.ds(pl.multiple_of(slot * rows, rows), rows)]

    def halves(ref, s):
        return ref.at[pl.ds(pl.multiple_of(s * half, half), half)]

    barrier = pltpu.get_barrier_semaphore()
    for zp in peers:
        pl.semaphore_signal(barrier, inc=1, device_id=(r, zp), device_id_type=MESH)
    pl.semaphore_signal(barrier, inc=1, device_id=(sib, z), device_id_type=MESH)

    pl.semaphore_signal(barrier, inc=1, device_id=(far, z), device_id_type=MESH)

    @pl.when(has_up)
    def _():
        pl.semaphore_signal(barrier, inc=1, device_id=(r + 2, z), device_id_type=MESH)

    @pl.when(has_dn)
    def _():
        pl.semaphore_signal(barrier, inc=1, device_id=(r - 2, z), device_id_type=MESH)

    columns = pl.ds(pl.multiple_of(z * quarter, quarter), quarter)
    own_copy = pltpu.make_async_copy(feats_ref.at[:, columns], panel(ext, 2), loc_sem)
    own_copy.start()
    own_copy.wait()
    pl.semaphore_wait(barrier, n_rep + 1 + has_up.astype(jnp.int32) + has_dn.astype(jnp.int32))

    own = panel(ext, 2)
    f_up = remote(own, panel(ext, 0), f_send.at[0], f_recv.at[0], (r + 2, z))
    f_dn = remote(own, panel(ext, 4), f_send.at[1], f_recv.at[1], (r - 2, z))
    f_sib = remote(own, panel(ext, 1 + 2 * k), f_send.at[2], f_recv.at[2], (sib, z))
    f_fwd = remote(
        panel(ext, 4 - 4 * k), panel(ext, 3 - 2 * k), f_send.at[3], f_recv.at[3], (sib, z)
    )
    from_dn = remote(own, panel(ext, 0), f_send.at[0], f_recv.at[0], (r - 2, z))
    from_up = remote(own, panel(ext, 4), f_send.at[1], f_recv.at[1], (r + 2, z))
    from_sib = remote(own, panel(ext, 3 - 2 * k), f_send.at[2], f_recv.at[2], (sib, z))
    from_fwd = remote(own, panel(ext, 1 + 2 * k), f_send.at[3], f_recv.at[3], (sib, z))
    fwd_out = jnp.where(k == 0, r + 2 < n_row, r >= 2)
    fwd_in = jnp.where(k == 0, r >= 2, r + 2 < n_row)

    @pl.when(has_up)
    def _():
        f_up.start()

    @pl.when(has_dn)
    def _():
        f_dn.start()

    f_sib.start()
    cot_out = [
        remote(halves(cot_ref, lax.rem(zp, 2)), cot_full.at[z], a_send.at[0, i], a_recv.at[0, i], (r, zp))
        for i, zp in enumerate(peers)
    ]
    eighth = feat // 8
    quad, pair = 4 * k, 4 * k + 2 * bit2

    def span(ref, start, count):
        return ref.at[pl.ds(pl.multiple_of(start * eighth, eighth), count * eighth)]

    def round_of(step, start, count, dev, first=False):
        ends = ((w_in_ref if first else w2_in, w2_in), (w_out_ref if first else w2_out, w2_out))
        return [
            remote(
                span(src, start, count), span(dst, start, count),
                w_send.at[2 * step + i], w_recv.at[2 * step + i], dev,
            )
            for i, (src, dst) in enumerate(ends)
        ]

    w_rounds = [
        round_of(0, pair + bit4, 1, (r, mate), True),
        round_of(1, pair + bit4, 1, (far, z)),
        round_of(2, pair, 2, (near, z)),
        round_of(3, quad, 4, (sib, z)),
    ]
    w_lands = [
        w_rounds[0],
        round_of(1, pair + 1 - bit4, 1, (far, z)),
        round_of(2, quad + 2 - 2 * bit2, 2, (near, z)),
        round_of(3, 4 - quad, 4, (sib, z)),
    ]

    def pass_weights(step):
        if step:
            for copy in w_lands[step - 1]:
                copy.wait_recv()
        if step < 4:
            for copy in w_rounds[step]:
                copy.start()

    pass_weights(0)

    @pl.when(jnp.logical_not(has_dn))
    def _():
        ext[0:rows] = jnp.zeros((rows, quarter), BF16)

    @pl.when(jnp.logical_not(has_up))
    def _():
        ext[4 * rows : 5 * rows] = jnp.zeros((rows, quarter), BF16)

    @pl.when(r < 1)
    def _():
        ext[rows : 2 * rows] = jnp.zeros((rows, quarter), BF16)

    @pl.when(r + 1 >= n_row)
    def _():
        ext[3 * rows : 4 * rows] = jnp.zeros((rows, quarter), BF16)

    cot_full[z] = cot_ref[pl.ds(pl.multiple_of(lax.rem(z, 2) * half, half), half), :]

    def transpose_block(b, carry):
        for s in range(slots):
            vals_t[b, s] = vals_ref[b, s].astype(F32).T.astype(BF16)
        return carry

    lax.fori_loop(0, row_blocks, transpose_block, 0)

    def fill_dense(t, carry):
        at = pl.ds(pl.multiple_of(t * 128, 128), 128)
        for b in range(row_blocks):
            straight = jnp.zeros((8, 16, 128), BF16)
            turned = jnp.zeros((8, 16, 128), BF16)
            for s in range(slots):
                row = mask_ref[t, b * slots + s : b * slots + s + 1, :]
                keep = jnp.broadcast_to(row, (16, 128)).astype(BF16)[None]
                straight = straight + vals_ref[b, s].reshape(8, 16, 128) * keep
                turned = turned + vals_t[b, s].reshape(8, 16, 128) * keep
            dense[b * 128 : (b + 1) * 128, at] = straight.reshape(128, 128)
            dense_t[at, b * 128 : (b + 1) * 128] = turned.reshape(128, 128)
        return carry

    lax.fori_loop(0, 5 * row_blocks, fill_dense, 0)
    pass_weights(1)
    for copy in cot_out:
        copy.start()

    def gather(slot, first=False):
        inner = pl.ds(pl.multiple_of(slot * rows, rows), rows)

        def step(m, carry):
            at = pl.ds(pl.multiple_of(m * 256, 256), 256)
            part = dot(dense[at, inner], ext[inner, :])
            agg_acc[at, :] = part if first else agg_acc[at, :] + part
            return carry

        lax.fori_loop(0, rows // 256, step, 0)

    gather(2, True)
    from_sib.wait_recv()
    gather(3 - 2 * k)

    @pl.when(has_dn)
    def _():
        from_dn.wait_recv()

    @pl.when(has_up)
    def _():
        from_up.wait_recv()

    @pl.when(fwd_out)
    def _():
        f_fwd.start()

    pass_weights(2)
    gather(0)
    gather(4)

    @pl.when(fwd_in)
    def _():
        from_fwd.wait_recv()

    gather(1 + 2 * k)
    agg[...] = agg_acc[...].astype(BF16)
    agg_out = [
        remote(halves(agg, lax.rem(zp, 2)), agg_full.at[z], a_send.at[1, i], a_recv.at[1, i], (r, zp))
        for i, zp in enumerate(peers)
    ]
    for copy in agg_out:
        copy.start()
    agg_full[z] = agg[pl.ds(pl.multiple_of(lax.rem(z, 2) * half, half), half), :]

    def arrivals(buf, kind):
        return [
            remote(buf.at[zf], buf.at[zf], a_send.at[kind, i], a_recv.at[kind, i], (r, zf))
            for i, zf in enumerate(froms)
        ]

    pass_weights(3)
    for copy in arrivals(cot_full, 0) + arrivals(agg_full, 1):
        copy.wait_recv()

    tile = 256

    def hidden_part(w_a, w_b, base):
        def step(i, carry):
            hc = pl.ds(pl.multiple_of(i * tile, tile), tile)
            to = pl.ds(pl.multiple_of(base + i * tile, tile), tile)
            wa, wb = w_a[:, hc], w_b[:, hc]
            for m in range(half // tile):
                rs = slice(m * tile, (m + 1) * tile)
                x = jnp.concatenate([agg_full[q, rs] for q in range(n_rep)], axis=1)
                c = jnp.concatenate([cot_full[q, rs] for q in range(n_rep)], axis=1)
                value, slope = gelu_pair(dot(x, wa))
                hid[rs, to] = value.astype(BF16)
                gp[rs, to] = (dot(c, wb) * slope).astype(BF16)
            return carry

        lax.fori_loop(0, hidw // tile, step, 0)

    hidden_part(w_in_ref, w_out_ref, 0)
    pass_weights(4)
    hidden_part(w2_in, w2_out, hidw)

    def product(src, w_a, w_b, dst, zq):
        at = pl.ds(pl.multiple_of(zq * quarter, quarter), quarter)
        wa, wb = w_a[at, :], w_b[at, :]
        for m in range(half // tile):
            rs = slice(m * tile, (m + 1) * tile)
            res = dot(src[rs, :hidw], wa, ((1,), (1,))) + dot(src[rs, hidw:], wb, ((1,), (1,)))
            dst[zq, rs] = res.astype(BF16)

    def to_peer(part, landing, kind, i):
        return remote(
            part.at[peers[i]], landing.at[z], a_send.at[kind, i], a_recv.at[kind, i], (r, peers[i])
        )

    adj_out = [to_peer(adj_p, adj_in, 2, i) for i in range(n_rep - 1)]
    out_out = [to_peer(out_p, out_in, 3, i) for i in range(n_rep - 1)]
    for i, zp in enumerate(peers):
        product(gp, w_in_ref, w2_in, adj_p, zp)
        adj_out[i].start()
    product(gp, w_in_ref, w2_in, adj_p, z)
    adj_in[z] = adj_p[z]
    for zp in peers + [z]:
        product(hid, w_out_ref, w2_out, out_p, zp)
    out_in[z] = out_p[z]

    for copy in arrivals(adj_in, 2):
        copy.wait_recv()
    for copy in out_out:
        copy.start()
    for s in range(2):
        total = adj_in[s].astype(F32)
        for q in range(s + 2, n_rep, 2):
            total = total + adj_in[q].astype(F32)
        adj[s * half : (s + 1) * half] = total.astype(BF16)

    def piece(p, m):
        at = pl.ds(pl.multiple_of(p * rows + m * tile, tile), tile)
        return dot(dense_t[at, :], adj[...])

    def put(p, slot):
        def step(m, carry):
            at = pl.ds(pl.multiple_of(m * tile, tile), tile)
            c_send[slot, at, :] = piece(p, m).astype(BF16)
            return carry

        lax.fori_loop(0, rows // tile, step, 0)

    plain_to, helped_to = r - 2 + 4 * k, r + 2 - 4 * k
    c_help = remote(c_send.at[0], c_sib.at[0], c_sends.at[0], c_recvs.at[0], (sib, z))
    c_own = remote(c_send.at[1], c_sib.at[1], c_sends.at[1], c_recvs.at[1], (sib, z))
    c_plain = remote(
        c_send.at[2], c_nbr.at[1 - k], c_sends.at[2], c_recvs.at[3 - k], (plain_to, z)
    )
    c_helped = remote(
        c_send.at[3], c_nbr.at[k], c_sends.at[3], c_recvs.at[2 + k], (helped_to, z)
    )
    put(1 + 2 * k, 0)
    c_help.start()
    put(4 * k, 2)
    plain_ok, helped_ok = fwd_in, fwd_out

    @pl.when(plain_ok)
    def _():
        c_plain.start()

    c_help.wait_recv()

    def add_help(m, carry):
        at = pl.ds(pl.multiple_of(m * tile, tile), tile)
        total = piece(4 - 4 * k, m) + c_sib[0, at, :].astype(F32)
        c_send[3, at, :] = total.astype(BF16)
        return carry

    lax.fori_loop(0, rows // tile, add_help, 0)

    @pl.when(helped_ok)
    def _():
        c_helped.start()

    put(3 - 2 * k, 1)
    c_own.start()

    for copy in arrivals(out_in, 3):
        copy.wait_recv()
    for s in range(2):
        total = out_in[s].astype(F32)
        for q in range(s + 2, n_rep, 2):
            total = total + out_in[q].astype(F32)
        mine = ext[2 * rows + s * half : 2 * rows + (s + 1) * half]
        upd_ref[s * half : (s + 1) * half] = (mine.astype(F32) + total).astype(BF16)

    c_own.wait_recv()
    from_low = remote(c_nbr.at[0], c_nbr.at[0], c_sends.at[2], c_recvs.at[2], (r - 2, z))
    from_high = remote(c_nbr.at[1], c_nbr.at[1], c_sends.at[3], c_recvs.at[3], (r + 2, z))

    @pl.when(has_dn)
    def _():
        from_low.wait_recv()

    @pl.when(jnp.logical_not(has_dn))
    def _():
        c_nbr[0] = jnp.zeros((rows, quarter), BF16)

    @pl.when(has_up)
    def _():
        from_high.wait_recv()

    @pl.when(jnp.logical_not(has_up))
    def _():
        c_nbr[1] = jnp.zeros((rows, quarter), BF16)

    def finish(m, carry):
        at = pl.ds(pl.multiple_of(m * tile, tile), tile)
        total = piece(2, m) + c_sib[1, at, :].astype(F32)
        total = total + c_nbr[0, at, :].astype(F32) + c_nbr[1, at, :].astype(F32)
        grad_ref[at, :] = (cot_ref[at, :].astype(F32) + total).astype(BF16)
        return carry

    lax.fori_loop(0, rows // tile, finish, 0)

    for copy in cot_out + sum(w_rounds, []) + agg_out + adj_out + out_out + [f_sib, c_help, c_own]:
        copy.wait_send()
    for ok, copy in (
        (has_up, f_up), (has_dn, f_dn), (fwd_out, f_fwd), (plain_ok, c_plain), (helped_ok, c_helped)
    ):
        pl.when(ok)(copy.wait_send)


def body(n_row, n_rep, node_feats, block_cols, block_vals, w_in, w_out, cotangent):
    rows, quarter = cotangent.shape
    feat = node_feats.shape[1]
    row_blocks, slots = block_cols.shape
    hidw = w_in.shape[1]
    half = rows // 2
    first = (lax.axis_index("row") - 2) * row_blocks
    position = jnp.where(block_cols >= 0, block_cols - first, -1).reshape(1, -1, 1)
    landing = jnp.arange(5 * row_blocks, dtype=jnp.int32).reshape(-1, 1, 1)
    mask = jnp.broadcast_to(
        (position == landing).astype(F32), (5 * row_blocks, row_blocks * slots, 128)
    )
    vmem = pl.BlockSpec(memory_space=pltpu.VMEM)
    dma = pltpu.SemaphoreType.DMA
    return pl.pallas_call(
        functools.partial(kernel, n_row, n_rep),
        out_shape=(jax.ShapeDtypeStruct((rows, quarter), BF16),) * 2,
        in_specs=[vmem, pl.BlockSpec(memory_space=pl.ANY), vmem, vmem, vmem, vmem],
        out_specs=(vmem, vmem),
        scratch_shapes=[
            pltpu.VMEM((5 * rows, quarter), BF16),
            pltpu.VMEM((row_blocks, slots, 128, 128), BF16),
            pltpu.VMEM((rows, 5 * rows), BF16),
            pltpu.VMEM((5 * rows, rows), BF16),
            pltpu.VMEM((rows, quarter), F32),
            pltpu.VMEM((feat, hidw), BF16),
            pltpu.VMEM((feat, hidw), BF16),
            pltpu.VMEM((n_rep, half, quarter), BF16),
            pltpu.VMEM((rows, quarter), BF16),
            pltpu.VMEM((n_rep, half, quarter), BF16),
            pltpu.VMEM((half, 2 * hidw), BF16),
            pltpu.VMEM((half, 2 * hidw), BF16),
            pltpu.VMEM((n_rep, half, quarter), BF16),
            pltpu.VMEM((n_rep, half, quarter), BF16),
            pltpu.VMEM((n_rep, half, quarter), BF16),
            pltpu.VMEM((n_rep, half, quarter), BF16),
            pltpu.VMEM((rows, quarter), BF16),
            pltpu.VMEM((4, rows, quarter), BF16),
            pltpu.VMEM((2, rows, quarter), BF16),
            pltpu.VMEM((2, rows, quarter), BF16),
            dma,
            dma((4,)),
            dma((4,)),
            dma((8,)),
            dma((8,)),
            dma((4, n_rep - 1)),
            dma((4, n_rep - 1)),
            dma((4,)),
            dma((4,)),
        ],
        compiler_params=pltpu.CompilerParams(
            collective_id=0, has_side_effects=True, vmem_limit_bytes=60 * 1024 * 1024
        ),
    )(mask, node_feats, block_vals, w_in, w_out, cotangent)


def solution(mesh):
    in_specs = (
        P("row", None),
        P("row", None),
        P("row", None, None, None),
        P(None, "rep"),
        P(None, "rep"),
        P("row", "rep"),
    )
    out_specs = (P("row", "rep"), P("row", "rep"))
    run = functools.partial(body, mesh.shape["row"], mesh.shape["rep"])
    return jax.shard_map(run, mesh=mesh, in_specs=in_specs, out_specs=out_specs, check_vma=False)
```
